256 devices in a mesh: dom: 64 (over y, z, core), col: 4 (over x).
Axes of the slice: x: 4, y: 4, z: 8, core: 2. Of those that a mesh axis runs over, the one named last changes fastest.
Arguments:
- blocks: bfloat16 [2048, 8, 128, 128], P(('dom', 'col')), as said below
- a_cols: int32 [2048, 8], P('dom'), may hold values from -1 to 47, as said below
- near_null: bfloat16 [2048, 32, 128], P('dom'), may hold values from -6 to 6
- owner: int32 [2048], P('dom'), may hold values from 0 to 15
- p_mask: int32 [2048, 3, 16], P('dom', None, 'col'), may hold values 0 or 1
- ghost_send: int32 [64, 2, 8], P('dom'), may hold values from -1 to 31, as said below
Outputs:
- prolongator: bfloat16 [262144, 3, 512], P('dom', None, 'col')
The draws below stay inside these ranges and needn't reach their ends.
Inputs may be any that keep to these rules, and one draw needn't show every extreme that they name: a_cols[r, 0] is r's own local index. Other entries: below 32 a block row of the same partition; 32 + s is slot s of ghost_send[d - 1, 1] of the partition before; 40 + s is slot s of ghost_send[d + 1, 0] of the partition after; -1 none. Referenced rows lie within 8 block rows of r, no column block is listed twice in a row, and every referenced slot holds a row. ghost_send[d, 0] lists, in slot order and packed at the front, block rows among the first 8 of partition d that partition d - 1 references; ghost_send[d, 1] those among the last 8 that partition d + 1 references; -1 fills empty slots; some partition fills all 8 slots. blocks[r, 0] has every diagonal entry at 0.5 or more.
All inputs are finite; a program needn't handle non-finite values. No bound on the sum of `p_mask` on one device may be relied on, other than what follows from the above.
Results may differ from the reference program's by a relative error of at most 0.0052.
Values may be sent and summed in bfloat16 or wider, within the bound.
A program may use at most 128 MiB of HBM per device.

```python
import jax
import jax.numpy as jnp
from jax import lax

BLK = 128
NV = 32
NAGG = 16
K = 8
SPAN = 8
SWEEPS = 3
RB_DEV = 32
RB_TOTAL = 2048
N_DOM = 64


def pattern_parts(key):
    offsets_all = jnp.concatenate([jnp.arange(-SPAN, 0), jnp.arange(1, SPAN + 1)]).astype(jnp.int32)
    positions = jnp.arange(2 * SPAN, dtype=jnp.int32)
    row_ids = jnp.arange(RB_DEV, dtype=jnp.int32)
    device_list = jnp.arange(N_DOM, dtype=jnp.int32)
    scores = jax.random.randint(jax.random.fold_in(key, 1), (N_DOM, RB_DEV, 2 * SPAN), 0, 1 << 16) * (2 * SPAN) + positions
    first_dev = jax.random.randint(jax.random.fold_in(key, 2), (), 1, N_DOM)
    left_force = (device_list[:, None] == first_dev) & (row_ids[None, :] < SPAN)
    right_force = (device_list[:, None] == first_dev - 1) & (row_ids[None, :] >= RB_DEV - SPAN)
    left_pos = SPAN - 1 - row_ids
    pinned = left_force[:, :, None] & (positions[None, None, :] == left_pos[None, :, None]) | right_force[:, :, None] & (positions[None, None, :] == 2 * SPAN - 1)
    scores = jnp.where(pinned, -1, scores)
    order = jnp.argsort(scores, axis=-1)[:, :, :K - 1]
    offsets = offsets_all[order]
    target = row_ids[None, :, None] + offsets
    remote = (target < 0) | (target >= RB_DEV)
    coin_flip = jax.random.randint(jax.random.fold_in(key, 3), (N_DOM, RB_DEV, K - 1), 0, 4)
    forced = (left_force | right_force)[:, :, None] & (jnp.arange(K - 1)[None, None, :] == 0)
    retained = (coin_flip < jnp.where(remote, 2, 3)) | forced
    device_ids = device_list[:, None, None]
    left_ref = retained & (target < 0) & (device_ids > 0)
    right_ref = retained & (target >= RB_DEV) & (device_ids < N_DOM - 1)
    local_ref = retained & (target >= 0) & (target < RB_DEV)
    candidates = jnp.arange(SPAN, dtype=jnp.int32)
    left_match = (target + SPAN)[..., None] == candidates
    right_match = (target - RB_DEV)[..., None] == candidates
    need_left = jnp.any(left_ref[..., None] & left_match, axis=(1, 2))
    need_right = jnp.any(right_ref[..., None] & right_match, axis=(1, 2))
    slot_left = jnp.cumsum(need_left.astype(jnp.int32), axis=1) - 1
    slot_right = jnp.cumsum(need_right.astype(jnp.int32), axis=1) - 1
    left_slot_of = jnp.sum(jnp.where(left_match, slot_left[:, None, None, :], 0), axis=-1)
    right_slot_of = jnp.sum(jnp.where(right_match, slot_right[:, None, None, :], 0), axis=-1)
    columns = jnp.where(local_ref, target, -1)
    columns = jnp.where(left_ref, RB_DEV + left_slot_of, columns)
    columns = jnp.where(right_ref, RB_DEV + SPAN + right_slot_of, columns)
    self_col = jnp.broadcast_to(row_ids[None, :, None], (N_DOM, RB_DEV, 1))
    a_cols = jnp.concatenate([self_col, columns], axis=2).reshape(N_DOM * RB_DEV, K).astype(jnp.int32)
    none_row = jnp.zeros((1, SPAN), dtype=bool)
    none_slot = jnp.zeros((1, SPAN), dtype=jnp.int32)
    need_first = jnp.concatenate([none_row, need_right[:-1]], axis=0)
    slot_first = jnp.concatenate([none_slot, slot_right[:-1]], axis=0)
    need_last = jnp.concatenate([need_left[1:], none_row], axis=0)
    slot_last = jnp.concatenate([slot_left[1:], none_slot], axis=0)

    def packed(needed, slot_of, base):
        match = needed[:, :, None] & (slot_of[:, :, None] == candidates[None, None, :])
        found = jnp.any(match, axis=1)
        chosen = jnp.sum(jnp.where(match, base + candidates[None, :, None], 0), axis=1)
        return jnp.where(found, chosen, -1)
    sends = jnp.stack([packed(need_first, slot_first, 0), packed(need_last, slot_last, RB_DEV - SPAN)], axis=1)
    return (a_cols, sends.astype(jnp.int32))


def draw_a_cols(key, part):
    return pattern_parts(key)[0]


def draw_ghost_send(key, part):
    return pattern_parts(key)[1]


def draw_blocks(key, part):
    key = jax.random.fold_in(key, 11)
    shape = (RB_DEV * N_DOM, K, BLK, BLK)
    scale = (BLK * K) ** (-0.5)
    first_key, second_key = jax.random.split(key)
    raw = jnp.clip(jax.random.normal(first_key, shape, jnp.float32), -4.0, 4.0)
    diagonal = jax.random.uniform(second_key, (RB_DEV * N_DOM, BLK), jnp.float32, 1.0, 2.0)
    identity = (jnp.arange(BLK)[:, None] == jnp.arange(BLK)[None, :]).astype(jnp.float32)
    leading = (jnp.arange(K) == 0).astype(jnp.float32)
    values = raw * scale + leading[None, :, None, None] * identity[None, None] * diagonal[:, None, :, None]
    return values.astype(jnp.bfloat16)


def place_ends(result, own_key, least, high):
    longest = result.shape.index(max(result.shape))
    spots = []
    for shift in (0, 1):
        where = [jax.random.randint(jax.random.fold_in(own_key, axis), (), 0, length) for axis, length in enumerate(result.shape)]
        where[longest] = (where[longest] + shift) % result.shape[longest]
        spots.append(tuple(where))
    return result.at[spots[0]].set(least).at[spots[1]].set(high)


def block_scale(key, extent, cuts, least, largest):
    gain, own = 1.0, jax.random.fold_in(key, 6)
    for dim, shards_of in cuts:
        draws = jnp.exp(jax.random.uniform(jax.random.fold_in(own, dim), (shards_of,), jnp.float32, least / len(cuts), largest / len(cuts)))
        gain = gain * jnp.repeat(draws, extent[dim] // shards_of).reshape([-1 if axis == dim else 1 for axis in range(len(extent))])
    return gain


def centred(rng, dims, scale, most, pieces=(), kind=jnp.bfloat16):
    result = jax.random.normal(rng, dims, jnp.float32) * scale
    if len(pieces) > 0:
        result = block_scale(rng, dims, pieces, -0.22, 0.18) * result
    return jnp.clip(result, min=-most, max=most).astype(kind)


def setup_inputs(seed: int = 0) -> dict:
    arg_keys = jax.random.split(jax.random.key(seed), 7)
    return {
        "blocks": draw_blocks(jax.random.fold_in(arg_keys[6], 71), 0),
        "a_cols": draw_a_cols(jax.random.fold_in(arg_keys[6], 71), 0),
        "near_null": centred(arg_keys[2], (RB_TOTAL, NV, BLK), 1.0, 6.0, ((0, 64),)),
        "owner": place_ends(jax.random.randint(arg_keys[3], (RB_TOTAL,), 0, NAGG), jax.random.fold_in(arg_keys[3], 1), 0, NAGG - 1).astype(jnp.int32),
        "p_mask": place_ends((jax.random.randint(arg_keys[4], (RB_TOTAL, 3, NAGG), 0, 2) < 1).astype(jnp.int32), jax.random.fold_in(arg_keys[4], 1), 0, 1),
        "ghost_send": draw_ghost_send(jax.random.fold_in(arg_keys[6], 71), 0),
    }


OMEGA = 2.0 / 3.0


def pick_rows(source, row_list):
    picked = jnp.take(source, jnp.clip(row_list, 0, source.shape[0] - 1).astype(jnp.int32), axis=0)
    return jnp.where((row_list >= 0)[:, None, None, None], picked, jnp.zeros_like(picked))


def partition_update(operands):
    local_p, left_in, right_in, local_blocks, local_cols, inverse_diag, pattern = operands
    empty_slot = jnp.zeros(left_in.shape[:2] + (1,) + left_in.shape[3:], jnp.bfloat16)
    extended = jnp.concatenate([
        local_p,
        jnp.concatenate([left_in, empty_slot], axis=2),
        jnp.concatenate([empty_slot, right_in], axis=2),
        jnp.zeros((1,) + local_p.shape[1:], jnp.bfloat16)], axis=0)
    column_index = jnp.where(local_cols < 0, extended.shape[0] - 1, local_cols).astype(jnp.int32)
    gathered = jnp.take(extended, column_index, axis=0).astype(jnp.float32)
    total = jnp.einsum("rkij,rkjwc->riwc", local_blocks.astype(jnp.float32), gathered)
    updated = local_p.astype(jnp.float32) - OMEGA * inverse_diag[:, :, None, None] * total
    return jnp.where(pattern, updated, 0.0).astype(jnp.bfloat16)


def reference(blocks, a_cols, near_null, owner, p_mask, ghost_send):
    block_rows = RB_DEV * N_DOM
    inverse_diag = 1.0 / jnp.diagonal(blocks[:, 0].astype(jnp.float32), axis1=1, axis2=2)
    aggregate_ids = jnp.arange(NAGG, dtype=jnp.int32)
    onehot = (owner[:, None] == aggregate_ids[None, :]).astype(jnp.float32)
    vectors = jnp.transpose(near_null, (0, 2, 1)).astype(jnp.float32)
    owned = (vectors[:, :, None, :] * onehot[:, None, :, None]).reshape(block_rows, BLK, NAGG * NV)
    empty = jnp.zeros_like(owned)
    prolong = jnp.stack([empty, owned, empty], axis=2).astype(jnp.bfloat16)
    middle = (jnp.arange(3) == 1)[None, :, None]
    allowed = (p_mask > 0) | (middle & (owner[:, None, None] == aggregate_ids[None, None, :]))
    pattern = jnp.repeat(allowed, NV, axis=2)[:, None]
    lead = (N_DOM, RB_DEV)
    blocks_dev = blocks.reshape(lead + blocks.shape[1:])
    cols_dev = a_cols.reshape(lead + a_cols.shape[1:])
    diag_dev = inverse_diag.reshape(lead + inverse_diag.shape[1:])
    pattern_dev = pattern.reshape(lead + pattern.shape[1:])
    for sweep_index in range(SWEEPS):
        per_device = prolong.reshape(lead + prolong.shape[1:])
        to_left = jax.vmap(pick_rows)(per_device[:, :, :, 0:2], ghost_send[:, 0])
        to_right = jax.vmap(pick_rows)(per_device[:, :, :, 1:3], ghost_send[:, 1])
        nothing = jnp.zeros_like(to_left[:1])
        left_in = jnp.concatenate([nothing, to_right[:-1]], axis=0)
        right_in = jnp.concatenate([to_left[1:], nothing], axis=0)
        updated = lax.map(partition_update, (per_device, left_in, right_in, blocks_dev, cols_dev, diag_dev, pattern_dev))
        prolong = updated.reshape(prolong.shape)
    return prolong.reshape(block_rows * BLK, 3, NAGG * NV)
```

```python
import jax
import jax.numpy as jnp
from jax import lax
from jax.experimental import pallas as pl
from jax.experimental.pallas import tpu as pltpu
from jax.sharding import PartitionSpec as P

OMEGA = 2.0 / 3.0
ROWS = 32
LISTED = 8
BLK = 128
COL = 4
GROUP = ROWS // COL
WIDTH = 2 * BLK
EMPTY = ROWS + 2 * GROUP
SLOTS = 12
AHEAD = 3
MESH = pl.DeviceIdType.MESH


def sent_row(group, position, leftward):
    first = 2 * position if not leftward else 2 * position + 1
    second = 2 * position - 7 if not leftward else 2 * position - 8
    place = jnp.where(position < 4, first, second)
    return group * GROUP + jnp.where(group < 2, place, GROUP - 1 - place)


def slot_row(sender, slot, leftward):
    forwards = (slot >= 3) & (slot <= 9) & (slot % 2 == 1)
    own = jnp.where(slot < 3, slot, jnp.where(slot == 11, 7, slot // 2 + 1))
    source = lax.rem(sender + jnp.where(leftward, 1, COL - 1), COL)
    group = jnp.where(forwards, source, sender)
    position = jnp.where(forwards, (slot - 3) // 2, own)
    return sent_row(group, position, leftward)


def kernel(
    cols, owner, mask_in, lists, blocks, vectors, out,
    held, p0, p1, p2, land0, land1, land2, scale, allow, stage, list_l, list_r, index_a, index_x, index_y,
    own_sem, send_sem, recv_sem, list_send, list_recv, ghost_send, ghost_recv, out_sem,
):
    pl.run_scoped(
        lambda *acc: body(
            cols, owner, mask_in, lists, blocks, vectors, out,
            held, p0, p1, p2, land0, land1, land2, scale, allow, stage, list_l, list_r, index_a, index_x, index_y,
            own_sem, send_sem, recv_sem, list_send, list_recv, ghost_send, ghost_recv, out_sem, acc,
        ),
        *[pltpu.ACC(mxu)((BLK, WIDTH), jnp.float32) for _ in range(2) for mxu in range(2)],
    )


def body(
    cols, owner, mask_in, lists, blocks, vectors, out,
    held, p0, p1, p2, land0, land1, land2, scale, allow, stage, list_l, list_r, index_a, index_x, index_y,
    own_sem, send_sem, recv_sem, list_send, list_recv, ghost_send, ghost_recv, out_sem, acc,
):
    me = lax.axis_index("col")
    part = lax.axis_index("dom")
    parts = lax.axis_size("dom")
    right, left = lax.rem(me + 1, COL), lax.rem(me + COL - 1, COL)
    after, before = lax.rem(part + 1, parts), lax.rem(part + parts - 1, parts)

    barrier = pltpu.get_barrier_semaphore()
    for axis, other in (("col", left), ("col", right), ("dom", before), ("dom", after)):
        pl.semaphore_signal(barrier, inc=1, device_id={axis: other}, device_id_type=MESH)
    pl.semaphore_wait(barrier, 4)

    own_copy = pltpu.make_async_copy(blocks, held.at[pl.ds(me * GROUP, GROUP)], own_sem)

    def gather_copy(slot, leftward, own):
        row = slot_row(me, slot, leftward)
        sem = (1 if leftward else 0), slot
        return pltpu.make_async_remote_copy(
            src_ref=blocks.at[row - me * GROUP] if own else held.at[row],
            dst_ref=held.at[row],
            send_sem=send_sem.at[sem],
            recv_sem=recv_sem.at[sem],
            device_id={"col": left if leftward else right},
            device_id_type=MESH,
        )

    def arrival(slot, leftward):
        row = slot_row(right if leftward else left, slot, leftward)
        sem = (1 if leftward else 0), slot
        return row, pltpu.make_async_remote_copy(
            src_ref=held.at[row],
            dst_ref=held.at[row],
            send_sem=send_sem.at[sem],
            recv_sem=recv_sem.at[sem],
            device_id={"col": left if leftward else right},
            device_id_type=MESH,
        )

    for slot in range(AHEAD):
        for leftward in (False, True):
            gather_copy(slot, leftward, True).start()
    own_copy.start()

    def list_copy(here, index, other):
        return pltpu.make_async_remote_copy(
            src_ref=lists,
            dst_ref=here,
            send_sem=list_send.at[index],
            recv_sem=list_recv.at[index],
            device_id={"dom": other},
            device_id_type=MESH,
        )

    list_copy(list_l, 0, after).start()
    list_copy(list_r, 1, before).start()

    def ghost_copy(source, target, sweep, row, place, count, other):
        src = source.at[pl.ds(row, count)] if count > 1 else source.at[row]
        dst = target.at[pl.ds(place, count)] if count > 1 else target.at[place]
        return pltpu.make_async_remote_copy(
            src_ref=src,
            dst_ref=dst,
            send_sem=ghost_send.at[sweep, place],
            recv_sem=ghost_recv.at[sweep, place],
            device_id={"dom": other},
            device_id_type=MESH,
        )

    @pl.loop(0, ROWS)
    def _(r):
        values = vectors[r].astype(jnp.float32)
        tall = jnp.concatenate([values] * 4, axis=0)
        aggregate = lax.broadcasted_iota(jnp.int32, (BLK, BLK), 0) // 32 + me * 4
        owned = jnp.where(aggregate == owner[r], tall, 0.0)
        middle = jnp.transpose(owned).astype(jnp.bfloat16)
        p0[r] = jnp.concatenate([jnp.zeros((BLK, BLK), jnp.bfloat16), middle], axis=1)

    ghost_copy(p0, land0, 0, 0, GROUP, GROUP, before).start()
    ghost_copy(p0, land0, 0, ROWS - GROUP, 0, GROUP, after).start()
    for buffer in (p0, p1, p2):
        buffer[EMPTY] = jnp.zeros((BLK, WIDTH), jnp.bfloat16)
    nothing = jnp.zeros((GROUP * BLK, BLK), jnp.bfloat16)
    stage[2, 0 : GROUP * BLK, :] = nothing
    stage[0, (ROWS - GROUP) * BLK : ROWS * BLK, :] = nothing

    lane = lax.broadcasted_iota(jnp.int32, (1, BLK), 1) // 32
    for half, order in ((0, (0, 1, 2)), (1, (2, 1, 0))):
        @pl.loop(half * ROWS // 2, (half + 1) * ROWS // 2)
        def _(r):
            pieces = []
            for w in order:
                piece = jnp.zeros((1, BLK), jnp.int32)
                for a in range(4):
                    value = mask_in[w, a, r]
                    if w == 1:
                        value = jnp.where(owner[r] == me * 4 + a, 1, value)
                    piece = jnp.where(lane == a, value, piece)
                pieces.append(piece)
            allow[r] = jnp.concatenate(pieces, axis=1)

    list_copy(list_l, 0, after).wait()
    list_copy(list_r, 1, before).wait()

    @pl.loop(0, ROWS)
    def _(r):
        for k in range(LISTED):
            c = cols[k, r]
            from_left = list_l[0, 1, jnp.clip(c - ROWS, 0, GROUP - 1)] - (ROWS - GROUP)
            from_right = list_r[0, 0, jnp.clip(c - ROWS - GROUP, 0, GROUP - 1)]
            from_left = jnp.where(from_left < 0, EMPTY, from_left + ROWS)
            from_right = jnp.where(from_right < 0, EMPTY, from_right + ROWS + GROUP)
            place = jnp.where(c < ROWS, c, jnp.where(c < ROWS + GROUP, from_left, from_right))
            place = jnp.where(c < 0, EMPTY, place)
            lower = (place < ROWS // 2) | ((place >= ROWS) & (place < ROWS + GROUP))
            index_a[r * LISTED + k] = place
            index_x[r * LISTED + k] = jnp.where(lower, place, EMPTY)
            index_y[r * LISTED + k] = jnp.where(lower, EMPTY, place)

    def settle(target, landed, place):
        value = landed[place]
        value = jnp.concatenate([value[:, BLK:], value[:, :BLK]], axis=1)
        exists = jnp.where(place < GROUP, part > 0, part < parts - 1)
        target[ROWS + place] = jnp.where(exists, value, jnp.zeros_like(value))

    ghost_copy(p0, land0, 0, 0, GROUP, GROUP, before).wait()
    ghost_copy(p0, land0, 0, ROWS - GROUP, 0, GROUP, after).wait()

    @pl.loop(0, 2 * GROUP)
    def _(place):
        settle(p0, land0, place)

    def issue(source, index, r, bank, mxu, q):
        def tile(k):
            return source[index[r * LISTED + k]]

        pltpu.matmul_push_rhs(jnp.concatenate([tile(2 * q), tile(2 * q + 1)], axis=0), q % 2, mxu)

    def multiply(r, bank, mxu, q):
        lhs = jnp.concatenate([held[r, 2 * q], held[r, 2 * q + 1]], axis=1)
        pltpu.matmul_acc_lhs(acc[2 * bank + mxu], lhs, load_staged_rhs=q % 2)

    def product(source, work, bank):
        for q in range(LISTED // 2):
            for mxu, (r, index) in enumerate(work):
                issue(source, index, r, bank, mxu, q)
            for mxu, (r, index) in enumerate(work):
                multiply(r, bank, mxu, q)

    def update(source, r, total):
        factor = scale[r]
        value = source[r].astype(jnp.float32) - jnp.concatenate([factor, factor], axis=1) * total
        return jnp.where(allow[r][:, :WIDTH] > 0, value, 0.0).astype(jnp.bfloat16)

    def make_scale(r):
        diagonal = lax.broadcasted_iota(jnp.int32, (BLK, BLK), 0) == lax.broadcasted_iota(jnp.int32, (BLK, BLK), 1)
        entries = jnp.sum(jnp.where(diagonal, held[r, 0].astype(jnp.float32), 0.0), axis=1, keepdims=True)
        scale[r] = jnp.broadcast_to(OMEGA * (1.0 / entries), (BLK, BLK))

    def sweep_rows(source, target, rows, after_row=None):
        pairs = [rows[i : i + 2] for i in range(0, len(rows), 2)]

        def finish(number):
            for mxu, r in enumerate(pairs[number]):
                target[r] = update(source, r, pltpu.matmul_pop(acc[2 * (number % 2) + mxu]))
                if after_row is not None:
                    after_row(r)

        for number, pair in enumerate(pairs):
            product(source, [(r, index_a) for r in pair], number % 2)
            if number > 0:
                finish(number - 1)
        finish(len(pairs) - 1)

    def send_ghost(source, landed, sweep):
        def start(r):
            @pl.when(r < GROUP)
            def _():
                ghost_copy(source, landed, sweep, r, GROUP + r, 1, before).start()

            @pl.when(r >= ROWS - GROUP)
            def _():
                ghost_copy(source, landed, sweep, r, r - (ROWS - GROUP), 1, after).start()

        return start

    own_copy.wait()

    @pl.loop(0, GROUP)
    def _(i):
        make_scale(me * GROUP + i)

    sweep_rows(p0, p1, [me * GROUP + i for i in range(GROUP)], send_ghost(p1, land1, 1))

    @pl.loop(0, SLOTS)
    def _(slot):
        row_l, copy_l = arrival(slot, False)
        row_r, copy_r = arrival(slot, True)
        copy_l.wait_recv()
        copy_r.wait_recv()
        later = slot + AHEAD
        forwards = (later <= 9) & (later % 2 == 1)

        @pl.when(forwards)
        def _():
            gather_copy(later, False, False).start()
            gather_copy(later, True, False).start()

        @pl.when((later < SLOTS) & jnp.logical_not(forwards))
        def _():
            gather_copy(later, False, True).start()
            gather_copy(later, True, True).start()

        make_scale(row_l)
        make_scale(row_r)
        sweep_rows(p0, p1, [row_l, row_r], send_ghost(p1, land1, 1))

    def settle_all(source, target, landed, sweep):
        @pl.loop(0, GROUP)
        def _(i):
            ghost_copy(source, landed, sweep, i, GROUP + i, 1, before).wait_recv()
            settle(target, landed, GROUP + i)
            ghost_copy(source, landed, sweep, ROWS - GROUP + i, i, 1, after).wait_recv()
            settle(target, landed, i)

    @pl.loop(GROUP, ROWS - GROUP, step=8)
    def _(r):
        sweep_rows(p1, p2, [r + i for i in range(8)])

    settle_all(p1, p1, land1, 1)

    @pl.loop(0, 2)
    def _(half):
        base = half * (ROWS - GROUP)
        sweep_rows(p1, p2, [base + i for i in range(8)], send_ghost(p2, land2, 2))

    def out_copy(w, r, count):
        place = pl.ds(pl.multiple_of(r * BLK, BLK), count * BLK)
        return pltpu.make_async_copy(stage.at[w, place], out.at[w, place], out_sem.at[w])

    def put(w, r, value):
        stage[w, pl.ds(pl.multiple_of(r * BLK, BLK), BLK), :] = value

    def inner_rows(rows, upper):
        near, far = (2, 0) if upper else (0, 2)

        def finish(number):
            r = rows[number]
            lower_sum = pltpu.matmul_pop(acc[2 * (number % 2)])
            upper_sum = pltpu.matmul_pop(acc[2 * (number % 2) + 1])
            middle = lower_sum[:, BLK:] + upper_sum[:, BLK:]
            near_sum, far_sum = (upper_sum, lower_sum) if upper else (lower_sum, upper_sum)
            factor = scale[r]
            old = p2[r].astype(jnp.float32)
            mask = allow[r]
            put(near, r, jnp.where(mask[:, :BLK] > 0, old[:, :BLK] - factor * near_sum[:, :BLK], 0.0).astype(jnp.bfloat16))
            put(1, r, jnp.where(mask[:, BLK:WIDTH] > 0, old[:, BLK:] - factor * middle, 0.0).astype(jnp.bfloat16))
            put(far, r, jnp.where(mask[:, WIDTH:] > 0, 0.0 - factor * far_sum[:, :BLK], 0.0).astype(jnp.bfloat16))

        for number, r in enumerate(rows):
            product(p2, [(r, index_x), (r, index_y)], number % 2)
            if number > 0:
                finish(number - 1)
        finish(len(rows) - 1)

    for upper in (False, True):
        @pl.loop(ROWS // 2 - GROUP + upper * GROUP, ROWS // 2 + upper * GROUP, step=4)
        def _(r):
            inner_rows([r + i for i in range(4)], upper)

    settle_all(p2, p2, land2, 2)

    def outer_rows(rows, outer):
        pairs = [rows[i : i + 2] for i in range(0, len(rows), 2)]

        def finish(number):
            for mxu, r in enumerate(pairs[number]):
                value = update(p2, r, pltpu.matmul_pop(acc[2 * (number % 2) + mxu]))
                put(outer, r, value[:, :BLK])
                put(1, r, value[:, BLK:])

        for number, pair in enumerate(pairs):
            product(p2, [(r, index_a) for r in pair], number % 2)
            if number > 0:
                finish(number - 1)
        finish(len(pairs) - 1)

    outer_rows([i for i in range(GROUP)], 0)
    outer_rows([ROWS - GROUP + i for i in range(GROUP)], 2)
    for w in range(3):
        out_copy(w, 0, ROWS).start()

    @pl.loop(0, SLOTS)
    def _(slot):
        forwards = (slot >= 3) & (slot <= 9) & (slot % 2 == 1)

        @pl.when(forwards)
        def _():
            gather_copy(slot, False, False).wait_send()
            gather_copy(slot, True, False).wait_send()

        @pl.when(jnp.logical_not(forwards))
        def _():
            gather_copy(slot, False, True).wait_send()
            gather_copy(slot, True, True).wait_send()

    @pl.loop(0, GROUP)
    def _(i):
        for source, landed, sweep in ((p1, land1, 1), (p2, land2, 2)):
            ghost_copy(source, landed, sweep, i, GROUP + i, 1, before).wait_send()
            ghost_copy(source, landed, sweep, ROWS - GROUP + i, i, 1, after).wait_send()

    for w in range(3):
        out_copy(w, 0, ROWS).wait()


def per_device(blocks, a_cols, near_null, owner, p_mask, ghost_send):
    scalar = pl.BlockSpec(memory_space=pltpu.SMEM)
    anywhere = pl.BlockSpec(memory_space=pl.ANY)
    dma = pltpu.SemaphoreType.DMA
    kept = pltpu.VMEM((EMPTY + 1, BLK, WIDTH), jnp.bfloat16)
    landing = pltpu.VMEM((2 * GROUP, BLK, WIDTH), jnp.bfloat16)
    index = pltpu.SMEM((ROWS * LISTED,), jnp.int32)
    result = pl.pallas_call(
        kernel,
        out_shape=jax.ShapeDtypeStruct((3, ROWS * BLK, BLK), jnp.bfloat16),
        in_specs=[scalar, scalar, scalar, anywhere, anywhere, pl.BlockSpec(memory_space=pltpu.VMEM)],
        out_specs=anywhere,
        scratch_shapes=[
            pltpu.VMEM((ROWS, LISTED, BLK, BLK), jnp.bfloat16),
            kept,
            kept,
            kept,
            landing,
            landing,
            landing,
            pltpu.VMEM((ROWS, BLK, BLK), jnp.float32),
            pltpu.VMEM((ROWS, 1, 3 * BLK), jnp.int32),
            pltpu.VMEM((3, ROWS * BLK, BLK), jnp.bfloat16),
            pltpu.SMEM((1, 2, GROUP), jnp.int32),
            pltpu.SMEM((1, 2, GROUP), jnp.int32),
            index,
            index,
            index,
            dma,
            dma((2, SLOTS)),
            dma((2, SLOTS)),
            dma((2,)),
            dma((2,)),
            dma((3, 2 * GROUP)),
            dma((3, 2 * GROUP)),
            dma((3,)),
        ],
        compiler_params=pltpu.CompilerParams(collective_id=0, has_side_effects=True, vmem_limit_bytes=48 << 20),
        cost_estimate=pl.CostEstimate(flops=10_000_000_000, bytes_accessed=16_000_000, transcendentals=0),
    )(a_cols.T, owner, p_mask.transpose(1, 2, 0), ghost_send, blocks, near_null)
    return result.transpose(1, 0, 2)


def solution(mesh):
    return jax.shard_map(
        per_device,
        mesh=mesh,
        in_specs=(
            P(("dom", "col"), None, None, None),
            P("dom", None),
            P("dom", None, None),
            P("dom"),
            P("dom", None, "col"),
            P("dom", None, None),
        ),
        out_specs=P("dom", None, "col"),
        check_vma=False,
    )
```

```python
import jax
import jax.numpy as jnp
from jax import lax
from jax.experimental import pallas as pl
from jax.experimental.pallas import tpu as pltpu
from jax.sharding import PartitionSpec as P

OMEGA = 2.0 / 3.0
ROWS = 32
LISTED = 8
BLK = 128
COL = 4
GROUP = ROWS // COL
WIDTH = 2 * BLK
EMPTY = ROWS + 2 * GROUP
SLOTS = 12
MESH = pl.DeviceIdType.MESH


def sent_row(group, position, leftward):
    first = 2 * position if not leftward else 2 * position + 1
    second = 2 * position - 7 if not leftward else 2 * position - 8
    place = jnp.where(position < 4, first, second)
    return group * GROUP + jnp.where(group < 2, place, GROUP - 1 - place)


def slot_row(sender, slot, leftward):
    forwards = slot >= GROUP
    source = lax.rem(sender + jnp.where(leftward, 1, COL - 1), COL)
    group = jnp.where(forwards, source, sender)
    position = jnp.where(forwards, slot - GROUP, slot)
    return sent_row(group, position, leftward)


def kernel(
    cols_in, owner_in, mask_at, lists, blocks, vectors_in, out,
    cols, owner, mask_in, vectors, in_sem, held, p0, p1, p2, land0, land1, land2, scale, allow, partial, list_l, list_r, index_a, index_x, index_y, find_a, find_b,
    own_sem, send_sem, recv_sem, list_send, list_recv, ghost_send, ghost_recv,
):
    pl.run_scoped(
        lambda *acc: body(
            cols_in, owner_in, mask_at, lists, blocks, vectors_in, out,
            cols, owner, mask_in, vectors, in_sem, held, p0, p1, p2, land0, land1, land2, scale, allow, partial, list_l, list_r, index_a, index_x, index_y, find_a, find_b,
            own_sem, send_sem, recv_sem, list_send, list_recv, ghost_send, ghost_recv, acc,
        ),
        *[pltpu.ACC(mxu)((BLK, WIDTH), jnp.float32) for _ in range(2) for mxu in range(2)],
    )


def body(
    cols_in, owner_in, mask_at, lists, blocks, vectors_in, out,
    cols, owner, mask_in, vectors, in_sem, held, p0, p1, p2, land0, land1, land2, scale, allow, partial, list_l, list_r, index_a, index_x, index_y, find_a, find_b,
    own_sem, send_sem, recv_sem, list_send, list_recv, ghost_send, ghost_recv, acc,
):
    me = lax.axis_index("col")
    part = lax.axis_index("dom")
    parts = lax.axis_size("dom")
    right, left = lax.rem(me + 1, COL), lax.rem(me + COL - 1, COL)
    after, before = lax.rem(part + 1, parts), lax.rem(part + parts - 1, parts)

    loads = [
        pltpu.make_async_copy(source, target, in_sem.at[number])
        for number, (source, target) in enumerate(
            ((vectors_in, vectors), (owner_in, owner), (mask_at, mask_in), (cols_in, cols))
        )
    ]
    for load in loads:
        load.start()
    barrier = pltpu.get_barrier_semaphore()
    for axis, other in (("col", left), ("col", right), ("dom", before), ("dom", after)):
        pl.semaphore_signal(barrier, inc=1, device_id={axis: other}, device_id_type=MESH)
    pl.semaphore_wait(barrier, 4)

    own_copy = pltpu.make_async_copy(blocks, held.at[pl.ds(me * GROUP, GROUP)], own_sem)

    def gather_copy(slot, leftward, own):
        row = slot_row(me, slot, leftward)
        sem = (1 if leftward else 0), slot
        return pltpu.make_async_remote_copy(
            src_ref=blocks.at[row - me * GROUP] if own else held.at[row],
            dst_ref=held.at[row],
            send_sem=send_sem.at[sem],
            recv_sem=recv_sem.at[sem],
            device_id={"col": left if leftward else right},
            device_id_type=MESH,
        )

    def arrival(slot, leftward):
        row = slot_row(right if leftward else left, slot, leftward)
        sem = (1 if leftward else 0), slot
        return row, pltpu.make_async_remote_copy(
            src_ref=held.at[row],
            dst_ref=held.at[row],
            send_sem=send_sem.at[sem],
            recv_sem=recv_sem.at[sem],
            device_id={"col": left if leftward else right},
            device_id_type=MESH,
        )

    for slot in range(GROUP):
        for leftward in (False, True):
            gather_copy(slot, leftward, True).start()
    own_copy.start()

    def list_copy(here, index, other):
        return pltpu.make_async_remote_copy(
            src_ref=lists,
            dst_ref=here,
            send_sem=list_send.at[index],
            recv_sem=list_recv.at[index],
            device_id={"dom": other},
            device_id_type=MESH,
        )

    list_copy(list_l, 0, after).start()
    list_copy(list_r, 1, before).start()

    def ghost_copy(source, target, sweep, row, place, count, other):
        src = source.at[pl.ds(row, count)] if count > 1 else source.at[row]
        dst = target.at[pl.ds(place, count)] if count > 1 else target.at[place]
        return pltpu.make_async_remote_copy(
            src_ref=src,
            dst_ref=dst,
            send_sem=ghost_send.at[sweep, place],
            recv_sem=ghost_recv.at[sweep, place],
            device_id={"dom": other},
            device_id_type=MESH,
        )

    for load in loads:
        load.wait()

    @pl.loop(0, ROWS)
    def _(r):
        values = vectors[r].astype(jnp.float32)
        tall = jnp.concatenate([values] * 4, axis=0)
        aggregate = lax.broadcasted_iota(jnp.int32, (BLK, BLK), 0) // 32 + me * 4
        owned = jnp.where(aggregate == owner[r], tall, 0.0)
        middle = jnp.transpose(owned).astype(jnp.bfloat16)
        p0[r] = jnp.concatenate([jnp.zeros((BLK, BLK), jnp.bfloat16), middle], axis=1)

    ghost_copy(p0, land0, 0, 0, GROUP, GROUP, before).start()
    ghost_copy(p0, land0, 0, ROWS - GROUP, 0, GROUP, after).start()
    for buffer in (p0, p1, p2):
        buffer[EMPTY] = jnp.zeros((BLK, WIDTH), jnp.bfloat16)
    held[ROWS, 0] = jnp.zeros((BLK, BLK), jnp.bfloat16)
    nothing = jnp.zeros((GROUP * BLK, BLK), jnp.bfloat16)
    out[2, 0 : GROUP * BLK, :] = nothing
    out[0, (ROWS - GROUP) * BLK : ROWS * BLK, :] = nothing

    late_pair = sent_row(lax.rem(me + 2, COL), SLOTS - GROUP - 1, False) // 2
    late_a, late_b = 2 * late_pair, 2 * late_pair + 1
    edge_pair = jnp.where(me == 2, ROWS // 2 - 1, 0)

    def other_pair(number, turn):
        first = lax.rem(late_pair + turn, ROWS // 2)
        second = lax.rem(edge_pair + turn, ROWS // 2)
        low, high = jnp.minimum(first, second), jnp.maximum(first, second)
        place = number + jnp.where(number >= low, 1, 0)
        place = place + jnp.where(place >= high, 1, 0)
        return lax.rem(place + ROWS // 2 - turn, ROWS // 2)

    lane = lax.broadcasted_iota(jnp.int32, (1, BLK), 1) // 32
    for half, order in ((0, (0, 1, 2)), (1, (2, 1, 0))):
        @pl.loop(half * ROWS // 2, (half + 1) * ROWS // 2)
        def _(r):
            pieces = []
            for w in order:
                piece = jnp.zeros((1, BLK), jnp.int32)
                for a in range(4):
                    value = mask_in[w, a, r]
                    if w == 1:
                        value = jnp.where(owner[r] == me * 4 + a, 1, value)
                    piece = jnp.where(lane == a, value, piece)
                pieces.append(piece)
            allow[r] = jnp.concatenate(pieces, axis=1)

    list_copy(list_l, 0, after).wait()
    list_copy(list_r, 1, before).wait()

    @pl.loop(0, ROWS)
    def _(r):
        found_a = jnp.int32(LISTED)
        found_b = jnp.int32(LISTED)
        for k in range(LISTED):
            c = cols[k, r]
            from_left = list_l[0, 1, jnp.clip(c - ROWS, 0, GROUP - 1)] - (ROWS - GROUP)
            from_right = list_r[0, 0, jnp.clip(c - ROWS - GROUP, 0, GROUP - 1)]
            from_left = jnp.where(from_left < 0, EMPTY, from_left + ROWS)
            from_right = jnp.where(from_right < 0, EMPTY, from_right + ROWS + GROUP)
            place = jnp.where(c < ROWS, c, jnp.where(c < ROWS + GROUP, from_left, from_right))
            place = jnp.where(c < 0, EMPTY, place)
            lower = (place < ROWS // 2) | ((place >= ROWS) & (place < ROWS + GROUP))
            index_a[r * LISTED + k] = place
            index_x[r * LISTED + k] = jnp.where(lower, place, EMPTY)
            index_y[r * LISTED + k] = jnp.where(lower, EMPTY, place)
            found_a = jnp.where(place == late_a, k, found_a)
            found_b = jnp.where(place == late_b, k, found_b)
        find_a[r] = found_a
        find_b[r] = found_b

    def settle(target, landed, place):
        value = landed[place]
        value = jnp.concatenate([value[:, BLK:], value[:, :BLK]], axis=1)
        exists = jnp.where(place < GROUP, part > 0, part < parts - 1)
        target[ROWS + place] = jnp.where(exists, value, jnp.zeros_like(value))

    ghost_copy(p0, land0, 0, 0, GROUP, GROUP, before).wait()
    ghost_copy(p0, land0, 0, ROWS - GROUP, 0, GROUP, after).wait()

    @pl.loop(0, 2 * GROUP)
    def _(place):
        settle(p0, land0, place)

    def issue(source, index, r, bank, mxu, q):
        def tile(k):
            return source[index[r * LISTED + k]]

        pltpu.matmul_push_rhs(jnp.concatenate([tile(2 * q), tile(2 * q + 1)], axis=0), q % 2, mxu)

    def multiply(r, bank, mxu, q):
        lhs = jnp.concatenate([held[r, 2 * q], held[r, 2 * q + 1]], axis=1)
        pltpu.matmul_acc_lhs(acc[2 * bank + mxu], lhs, load_staged_rhs=q % 2)

    def product(source, work, bank):
        for q in range(LISTED // 2):
            for mxu, (r, index) in enumerate(work):
                issue(source, index, r, bank, mxu, q)
            for mxu, (r, index) in enumerate(work):
                multiply(r, bank, mxu, q)

    def update(source, r, total):
        factor = scale[r]
        value = source[r].astype(jnp.float32) - jnp.concatenate([factor, factor], axis=1) * total
        return jnp.where(allow[r][:, :WIDTH] > 0, value, 0.0).astype(jnp.bfloat16)

    def make_scale(r):
        diagonal = lax.broadcasted_iota(jnp.int32, (BLK, BLK), 0) == lax.broadcasted_iota(jnp.int32, (BLK, BLK), 1)
        entries = jnp.sum(jnp.where(diagonal, held[r, 0].astype(jnp.float32), 0.0), axis=1, keepdims=True)
        scale[r] = jnp.broadcast_to(OMEGA * (1.0 / entries), (BLK, BLK))

    def sweep_rows(source, target, rows, after_row=None):
        pairs = [rows[i : i + 2] for i in range(0, len(rows), 2)]

        def finish(number):
            for mxu, r in enumerate(pairs[number]):
                target[r] = update(source, r, pltpu.matmul_pop(acc[2 * (number % 2) + mxu]))

        for number, pair in enumerate(pairs):
            product(source, [(r, index_a) for r in pair], number % 2)
            if number > 0:
                finish(number - 1)
        finish(len(pairs) - 1)
        if after_row is not None:
            for r in rows:
                after_row(r)

    def send_ghost(source, landed, sweep):
        def start(r):
            @pl.when(r < GROUP)
            def _():
                ghost_copy(source, landed, sweep, r, GROUP + r, 1, before).start()

            @pl.when(r >= ROWS - GROUP)
            def _():
                ghost_copy(source, landed, sweep, r, r - (ROWS - GROUP), 1, after).start()

        return start

    own_copy.wait()

    @pl.loop(0, GROUP)
    def _(i):
        make_scale(me * GROUP + i)

    sweep_rows(p0, p1, [me * GROUP + i for i in range(GROUP)], send_ghost(p1, land1, 1))

    def receive(slot):
        row_l, copy_l = arrival(slot, False)
        row_r, copy_r = arrival(slot, True)
        copy_l.wait_recv()
        copy_r.wait_recv()
        return row_l, row_r

    def first_sweep(row_l, row_r):
        make_scale(row_l)
        make_scale(row_r)
        sweep_rows(p0, p1, [row_l, row_r], send_ghost(p1, land1, 1))

    p1[late_a] = jnp.zeros((BLK, WIDTH), jnp.bfloat16)
    p1[late_b] = jnp.zeros((BLK, WIDTH), jnp.bfloat16)

    @pl.loop(0, SLOTS - GROUP)
    def _(slot):
        rows = receive(slot)
        gather_copy(slot + GROUP, False, False).start()
        gather_copy(slot + GROUP, True, False).start()
        first_sweep(*rows)

    @pl.loop(SLOTS - GROUP, SLOTS - 1)
    def _(slot):
        first_sweep(*receive(slot))

    def take_ghost(source, landed, sweep, place):
        @pl.when(place < GROUP)
        def _():
            ghost_copy(source, landed, sweep, ROWS - GROUP + place, place, 1, after).wait_recv()

        @pl.when(place >= GROUP)
        def _():
            ghost_copy(source, landed, sweep, place - GROUP, place, 1, before).wait_recv()

        settle(source, landed, place)

    def partial_rows(numbers):
        pairs = [other_pair(number, ROWS // 2 - 4) for number in numbers]

        def finish(number):
            for mxu in range(2):
                partial[2 * pairs[number] + mxu] = pltpu.matmul_pop(acc[2 * (number % 2) + mxu])

        for number, pair in enumerate(pairs):
            product(p1, [(2 * pair, index_a), (2 * pair + 1, index_a)], number % 2)
            if number > 0:
                finish(number - 1)
        finish(len(pairs) - 1)

    late_ghost = jnp.where(me == 2, 2 * GROUP - 2, 0)
    p1[ROWS + late_ghost] = jnp.zeros((BLK, WIDTH), jnp.bfloat16)
    p1[ROWS + late_ghost + 1] = jnp.zeros((BLK, WIDTH), jnp.bfloat16)
    partial_rows(range(7))

    @pl.loop(0, 2 * GROUP - 2)
    def _(i):
        take_ghost(p1, land1, 1, i + jnp.where(me == 2, 0, 2))

    partial_rows(range(7, 14))
    first_sweep(*receive(SLOTS - 1))

    send_second = send_ghost(p2, land2, 2)
    sweep_rows(p1, p2, [late_a, late_b], send_second)

    def corrected_rows(numbers):
        pairs = [other_pair(number, 4) for number in numbers]

        def finish(number):
            for mxu in range(2):
                r = 2 * pairs[number] + mxu
                total = partial[r] + pltpu.matmul_pop(acc[2 * (number % 2) + mxu])
                p2[r] = update(p1, r, total)

        tile = jnp.concatenate([p1[late_a], p1[late_b]], axis=0)
        for mxu in range(2):
            pltpu.matmul_push_rhs(tile, 0, mxu)
        for number, pair in enumerate(pairs):
            for mxu in range(2):
                r = 2 * pair + mxu
                k_a, k_b = find_a[r], find_b[r]
                lhs = [held[jnp.where(k < LISTED, r, ROWS), jnp.where(k < LISTED, k, 0)] for k in (k_a, k_b)]
                pltpu.matmul_acc_lhs(
                    acc[2 * (number % 2) + mxu],
                    jnp.concatenate(lhs, axis=1),
                    load_staged_rhs=0 if number == 0 else None,
                )
            if number > 0:
                finish(number - 1)
        finish(len(pairs) - 1)
        if numbers[0] < 7:
            for pair in pairs:
                send_second(2 * pair)
                send_second(2 * pair + 1)

    corrected_rows(range(4))
    corrected_rows(range(4, 7))
    corrected_rows(range(7, 14))
    take_ghost(p1, land1, 1, late_ghost)
    take_ghost(p1, land1, 1, late_ghost + 1)
    sweep_rows(p1, p2, [2 * edge_pair, 2 * edge_pair + 1], send_second)

    def put(w, r, value):
        out[w, pl.ds(pl.multiple_of(r * BLK, BLK), BLK), :] = value

    def inner_rows(rows, upper):
        near, far = (2, 0) if upper else (0, 2)

        def finish(number):
            r = rows[number]
            lower_sum = pltpu.matmul_pop(acc[2 * (number % 2)])
            upper_sum = pltpu.matmul_pop(acc[2 * (number % 2) + 1])
            middle = lower_sum[:, BLK:] + upper_sum[:, BLK:]
            near_sum, far_sum = (upper_sum, lower_sum) if upper else (lower_sum, upper_sum)
            factor = scale[r]
            old = p2[r].astype(jnp.float32)
            mask = allow[r]
            put(near, r, jnp.where(mask[:, :BLK] > 0, old[:, :BLK] - factor * near_sum[:, :BLK], 0.0).astype(jnp.bfloat16))
            put(1, r, jnp.where(mask[:, BLK:WIDTH] > 0, old[:, BLK:] - factor * middle, 0.0).astype(jnp.bfloat16))
            put(far, r, jnp.where(mask[:, WIDTH:] > 0, 0.0 - factor * far_sum[:, :BLK], 0.0).astype(jnp.bfloat16))

        for number, r in enumerate(rows):
            product(p2, [(r, index_x), (r, index_y)], number % 2)
            if number > 0:
                finish(number - 1)
        finish(len(rows) - 1)

    for upper in (False, True):
        @pl.loop(ROWS // 2 - GROUP + upper * GROUP, ROWS // 2 + upper * GROUP, step=4)
        def _(r):
            inner_rows([r + i for i in range(4)], upper)

    def outer_rows(rows, outer):
        pairs = [rows[i : i + 2] for i in range(0, len(rows), 2)]

        def finish(number):
            for mxu, r in enumerate(pairs[number]):
                value = update(p2, r, pltpu.matmul_pop(acc[2 * (number % 2) + mxu]))
                put(outer, r, value[:, :BLK])
                put(1, r, value[:, BLK:])

        for number, pair in enumerate(pairs):
            product(p2, [(r, index_a) for r in pair], number % 2)
            if number > 0:
                finish(number - 1)
        finish(len(pairs) - 1)

    @pl.loop(0, 2)
    def _(number):
        upper = jnp.where(me == 2, number, 1 - number)

        @pl.loop(0, GROUP)
        def _(i):
            take_ghost(p2, land2, 2, upper * GROUP + i)

        outer_rows([upper * (ROWS - GROUP) + i for i in range(GROUP)], 2 * upper)

    @pl.loop(0, SLOTS)
    def _(slot):
        @pl.when(slot >= GROUP)
        def _():
            gather_copy(slot, False, False).wait_send()
            gather_copy(slot, True, False).wait_send()

        @pl.when(slot < GROUP)
        def _():
            gather_copy(slot, False, True).wait_send()
            gather_copy(slot, True, True).wait_send()

    @pl.loop(0, GROUP)
    def _(i):
        for source, landed, sweep in ((p1, land1, 1), (p2, land2, 2)):
            ghost_copy(source, landed, sweep, i, GROUP + i, 1, before).wait_send()
            ghost_copy(source, landed, sweep, ROWS - GROUP + i, i, 1, after).wait_send()


def per_device(blocks, a_cols, near_null, owner, p_mask, ghost_send):
    hbm = pl.BlockSpec(memory_space=pltpu.HBM)
    dma = pltpu.SemaphoreType.DMA
    kept = pltpu.VMEM((EMPTY + 1, BLK, WIDTH), jnp.bfloat16)
    landing = pltpu.VMEM((2 * GROUP, BLK, WIDTH), jnp.bfloat16)
    index = pltpu.SMEM((ROWS * LISTED,), jnp.int32)
    result = pl.pallas_call(
        kernel,
        out_shape=pltpu.VMEM((3, ROWS * BLK, BLK), jnp.bfloat16),
        in_specs=[hbm] * 6,
        out_specs=pl.BlockSpec(memory_space=pltpu.VMEM),
        scratch_shapes=[
            pltpu.SMEM((LISTED, ROWS), jnp.int32),
            pltpu.SMEM((ROWS,), jnp.int32),
            pltpu.SMEM((3, 4, ROWS), jnp.int32),
            pltpu.VMEM((ROWS, 32, BLK), jnp.bfloat16),
            dma((4,)),
            pltpu.VMEM((ROWS + 1, LISTED, BLK, BLK), jnp.bfloat16),
            kept,
            kept,
            kept,
            landing,
            landing,
            landing,
            pltpu.VMEM((ROWS, BLK, BLK), jnp.float32),
            pltpu.VMEM((ROWS, 1, 3 * BLK), jnp.int32),
            pltpu.VMEM((ROWS, BLK, WIDTH), jnp.float32),
            pltpu.SMEM((1, 2, GROUP), jnp.int32),
            pltpu.SMEM((1, 2, GROUP), jnp.int32),
            index,
            index,
            index,
            pltpu.SMEM((ROWS,), jnp.int32),
            pltpu.SMEM((ROWS,), jnp.int32),
            dma,
            dma((2, SLOTS)),
            dma((2, SLOTS)),
            dma((2,)),
            dma((2,)),
            dma((3, 2 * GROUP)),
            dma((3, 2 * GROUP)),
        ],
        compiler_params=pltpu.CompilerParams(collective_id=0, has_side_effects=True, vmem_limit_bytes=60 << 20),
        cost_estimate=pl.CostEstimate(flops=10_000_000_000, bytes_accessed=16_000_000, transcendentals=0),
    )(a_cols.T, owner, p_mask.transpose(1, 2, 0), ghost_send, blocks, near_null)
    return result.transpose(1, 0, 2)


def solution(mesh):
    return jax.shard_map(
        per_device,
        mesh=mesh,
        in_specs=(
            P(("dom", "col"), None, None, None),
            P("dom", None),
            P("dom", None, None),
            P("dom"),
            P("dom", None, "col"),
            P("dom", None, None),
        ),
        out_specs=P("dom", None, "col"),
        check_vma=False,
    )
```

```python
import jax
import jax.numpy as jnp
from jax import lax
from jax.experimental import pallas as pl
from jax.experimental.pallas import tpu as pltpu
from jax.sharding import PartitionSpec as P

OMEGA = 2.0 / 3.0
ROWS = 32
LISTED = 8
BLK = 128
COL = 4
GROUP = ROWS // COL
WIDTH = 2 * BLK
EMPTY = ROWS + 2 * GROUP
SLOTS = 12
AHEAD = 4
MESH = pl.DeviceIdType.MESH


def sent_row(group, position, leftward):
    first = 2 * position if not leftward else 2 * position + 1
    second = 2 * position - 7 if not leftward else 2 * position - 8
    place = jnp.where(position < 4, first, second)
    return group * GROUP + jnp.where(group < 2, place, GROUP - 1 - place)


def is_forward(slot):
    return (slot == 4) | (slot == 6) | (slot >= SLOTS - 2)


def slot_row(sender, slot, leftward):
    forwards = is_forward(slot)
    source = lax.rem(sender + jnp.where(leftward, 1, COL - 1), COL)
    group = jnp.where(forwards, source, sender)
    own = jnp.where(slot < 4, slot, jnp.where(slot == 5, 4, slot - 2))
    passed = jnp.where(slot < SLOTS - 2, slot // 2 - 2, slot - GROUP)
    position = jnp.where(forwards, passed, own)
    return sent_row(group, position, leftward)


def kernel(
    cols_in, owner_in, mask_at, lists, blocks, vectors_in, out,
    cols, owner, mask_in, vectors, in_sem, held, p0, p1, p2, land0, land1, land2, scale, allow, partial, list_l, list_r, index_a, index_x, index_y, find_a, find_b,
    own_sem, send_sem, recv_sem, list_send, list_recv, ghost_send, ghost_recv,
):
    pl.run_scoped(
        lambda *acc: body(
            cols_in, owner_in, mask_at, lists, blocks, vectors_in, out,
            cols, owner, mask_in, vectors, in_sem, held, p0, p1, p2, land0, land1, land2, scale, allow, partial, list_l, list_r, index_a, index_x, index_y, find_a, find_b,
            own_sem, send_sem, recv_sem, list_send, list_recv, ghost_send, ghost_recv, acc,
        ),
        *[pltpu.ACC(mxu)((BLK, WIDTH), jnp.float32) for _ in range(2) for mxu in range(2)],
    )


def body(
    cols_in, owner_in, mask_at, lists, blocks, vectors_in, out,
    cols, owner, mask_in, vectors, in_sem, held, p0, p1, p2, land0, land1, land2, scale, allow, partial, list_l, list_r, index_a, index_x, index_y, find_a, find_b,
    own_sem, send_sem, recv_sem, list_send, list_recv, ghost_send, ghost_recv, acc,
):
    me = lax.axis_index("col")
    part = lax.axis_index("dom")
    parts = lax.axis_size("dom")
    right, left = lax.rem(me + 1, COL), lax.rem(me + COL - 1, COL)
    after, before = lax.rem(part + 1, parts), lax.rem(part + parts - 1, parts)

    loads = [
        pltpu.make_async_copy(source, target, in_sem.at[number])
        for number, (source, target) in enumerate(
            ((vectors_in, vectors), (owner_in, owner), (mask_at, mask_in), (cols_in, cols))
        )
    ]
    for load in loads:
        load.start()
    barrier = pltpu.get_barrier_semaphore()
    for axis, other in (("col", left), ("col", right), ("dom", before), ("dom", after)):
        pl.semaphore_signal(barrier, inc=1, device_id={axis: other}, device_id_type=MESH)
    pl.semaphore_wait(barrier, 4)

    own_copy = pltpu.make_async_copy(blocks, held.at[pl.ds(me * GROUP, GROUP)], own_sem)

    def gather_copy(slot, leftward, own):
        row = slot_row(me, slot, leftward)
        sem = (1 if leftward else 0), slot
        return pltpu.make_async_remote_copy(
            src_ref=blocks.at[row - me * GROUP] if own else held.at[row],
            dst_ref=held.at[row],
            send_sem=send_sem.at[sem],
            recv_sem=recv_sem.at[sem],
            device_id={"col": left if leftward else right},
            device_id_type=MESH,
        )

    def arrival(slot, leftward):
        row = slot_row(right if leftward else left, slot, leftward)
        sem = (1 if leftward else 0), slot
        return row, pltpu.make_async_remote_copy(
            src_ref=held.at[row],
            dst_ref=held.at[row],
            send_sem=send_sem.at[sem],
            recv_sem=recv_sem.at[sem],
            device_id={"col": left if leftward else right},
            device_id_type=MESH,
        )

    for slot in range(AHEAD):
        for leftward in (False, True):
            gather_copy(slot, leftward, True).start()
    own_copy.start()

    def list_copy(here, index, other):
        return pltpu.make_async_remote_copy(
            src_ref=lists,
            dst_ref=here,
            send_sem=list_send.at[index],
            recv_sem=list_recv.at[index],
            device_id={"dom": other},
            device_id_type=MESH,
        )

    list_copy(list_l, 0, after).start()
    list_copy(list_r, 1, before).start()

    def ghost_copy(source, target, sweep, row, place, count, other):
        src = source.at[pl.ds(row, count)] if count > 1 else source.at[row]
        dst = target.at[pl.ds(place, count)] if count > 1 else target.at[place]
        return pltpu.make_async_remote_copy(
            src_ref=src,
            dst_ref=dst,
            send_sem=ghost_send.at[sweep, place],
            recv_sem=ghost_recv.at[sweep, place],
            device_id={"dom": other},
            device_id_type=MESH,
        )

    for load in loads:
        load.wait()

    @pl.loop(0, ROWS)
    def _(r):
        values = vectors[r].astype(jnp.float32)
        tall = jnp.concatenate([values] * 4, axis=0)
        aggregate = lax.broadcasted_iota(jnp.int32, (BLK, BLK), 0) // 32 + me * 4
        owned = jnp.where(aggregate == owner[r], tall, 0.0)
        middle = jnp.transpose(owned).astype(jnp.bfloat16)
        p0[r] = jnp.concatenate([jnp.zeros((BLK, BLK), jnp.bfloat16), middle], axis=1)

    ghost_copy(p0, land0, 0, 0, GROUP, GROUP, before).start()
    ghost_copy(p0, land0, 0, ROWS - GROUP, 0, GROUP, after).start()
    for buffer in (p0, p1, p2):
        buffer[EMPTY] = jnp.zeros((BLK, WIDTH), jnp.bfloat16)
    held[ROWS, 0] = jnp.zeros((BLK, BLK), jnp.bfloat16)
    nothing = jnp.zeros((GROUP * BLK, BLK), jnp.bfloat16)
    out[2, 0 : GROUP * BLK, :] = nothing
    out[0, (ROWS - GROUP) * BLK : ROWS * BLK, :] = nothing

    late_pair = sent_row(lax.rem(me + 2, COL), SLOTS - GROUP - 1, False) // 2
    late_a, late_b = 2 * late_pair, 2 * late_pair + 1
    edge_pair = jnp.where(me == 2, ROWS // 2 - 2, 0)

    def other_pair(number, turn):
        first = lax.rem(late_pair + turn, ROWS // 2)
        second = lax.rem(edge_pair + turn, ROWS // 2)
        low = jnp.minimum(first, second)
        high = jnp.maximum(first, second)
        place = number + jnp.where(number >= low, jnp.where(second < first, 2, 1), 0)
        place = place + jnp.where(place >= high, jnp.where(second < first, 1, 2), 0)
        return lax.rem(place + ROWS // 2 - turn, ROWS // 2)

    lane = lax.broadcasted_iota(jnp.int32, (1, BLK), 1) // 32
    for half, order in ((0, (0, 1, 2)), (1, (2, 1, 0))):
        @pl.loop(half * ROWS // 2, (half + 1) * ROWS // 2)
        def _(r):
            pieces = []
            for w in order:
                piece = jnp.zeros((1, BLK), jnp.int32)
                for a in range(4):
                    value = mask_in[w, a, r]
                    if w == 1:
                        value = jnp.where(owner[r] == me * 4 + a, 1, value)
                    piece = jnp.where(lane == a, value, piece)
                pieces.append(piece)
            allow[r] = jnp.concatenate(pieces, axis=1)

    list_copy(list_l, 0, after).wait()
    list_copy(list_r, 1, before).wait()

    @pl.loop(0, ROWS)
    def _(r):
        found_a = jnp.int32(LISTED)
        found_b = jnp.int32(LISTED)
        for k in range(LISTED):
            c = cols[k, r]
            from_left = list_l[0, 1, jnp.clip(c - ROWS, 0, GROUP - 1)] - (ROWS - GROUP)
            from_right = list_r[0, 0, jnp.clip(c - ROWS - GROUP, 0, GROUP - 1)]
            from_left = jnp.where(from_left < 0, EMPTY, from_left + ROWS)
            from_right = jnp.where(from_right < 0, EMPTY, from_right + ROWS + GROUP)
            place = jnp.where(c < ROWS, c, jnp.where(c < ROWS + GROUP, from_left, from_right))
            place = jnp.where(c < 0, EMPTY, place)
            lower = (place < ROWS // 2) | ((place >= ROWS) & (place < ROWS + GROUP))
            index_a[r * LISTED + k] = place
            index_x[r * LISTED + k] = jnp.where(lower, place, EMPTY)
            index_y[r * LISTED + k] = jnp.where(lower, EMPTY, place)
            found_a = jnp.where(place == late_a, k, found_a)
            found_b = jnp.where(place == late_b, k, found_b)
        find_a[r] = found_a
        find_b[r] = found_b

    def settle(target, landed, place):
        value = landed[place]
        value = jnp.concatenate([value[:, BLK:], value[:, :BLK]], axis=1)
        exists = jnp.where(place < GROUP, part > 0, part < parts - 1)
        target[ROWS + place] = jnp.where(exists, value, jnp.zeros_like(value))

    ghost_copy(p0, land0, 0, 0, GROUP, GROUP, before).wait()
    ghost_copy(p0, land0, 0, ROWS - GROUP, 0, GROUP, after).wait()

    @pl.loop(0, 2 * GROUP)
    def _(place):
        settle(p0, land0, place)

    def issue(source, index, r, bank, mxu, q):
        def tile(k):
            return source[index[r * LISTED + k]]

        pltpu.matmul_push_rhs(jnp.concatenate([tile(2 * q), tile(2 * q + 1)], axis=0), q % 2, mxu)

    def multiply(r, bank, mxu, q):
        lhs = jnp.concatenate([held[r, 2 * q], held[r, 2 * q + 1]], axis=1)
        pltpu.matmul_acc_lhs(acc[2 * bank + mxu], lhs, load_staged_rhs=q % 2)

    def product(source, work, bank):
        for q in range(LISTED // 2):
            for mxu, (r, index) in enumerate(work):
                issue(source, index, r, bank, mxu, q)
            for mxu, (r, index) in enumerate(work):
                multiply(r, bank, mxu, q)

    def update(source, r, total):
        factor = scale[r]
        value = source[r].astype(jnp.float32) - jnp.concatenate([factor, factor], axis=1) * total
        return jnp.where(allow[r][:, :WIDTH] > 0, value, 0.0).astype(jnp.bfloat16)

    def make_scale(r):
        diagonal = lax.broadcasted_iota(jnp.int32, (BLK, BLK), 0) == lax.broadcasted_iota(jnp.int32, (BLK, BLK), 1)
        entries = jnp.sum(jnp.where(diagonal, held[r, 0].astype(jnp.float32), 0.0), axis=1, keepdims=True)
        scale[r] = jnp.broadcast_to(OMEGA * (1.0 / entries), (BLK, BLK))

    def sweep_rows(source, target, rows, after_row=None):
        pairs = [rows[i : i + 2] for i in range(0, len(rows), 2)]

        def finish(number):
            for mxu, r in enumerate(pairs[number]):
                target[r] = update(source, r, pltpu.matmul_pop(acc[2 * (number % 2) + mxu]))

        for number, pair in enumerate(pairs):
            product(source, [(r, index_a) for r in pair], number % 2)
            if number > 0:
                finish(number - 1)
        finish(len(pairs) - 1)
        if after_row is not None:
            for r in rows:
                after_row(r)

    def send_ghost(source, landed, sweep):
        def start(r):
            @pl.when(r < GROUP)
            def _():
                ghost_copy(source, landed, sweep, r, GROUP + r, 1, before).start()

            @pl.when(r >= ROWS - GROUP)
            def _():
                ghost_copy(source, landed, sweep, r, r - (ROWS - GROUP), 1, after).start()

        return start

    own_copy.wait()

    @pl.loop(0, GROUP)
    def _(i):
        make_scale(me * GROUP + i)

    sweep_rows(p0, p1, [me * GROUP + i for i in range(GROUP)], send_ghost(p1, land1, 1))

    def receive(slot):
        row_l, copy_l = arrival(slot, False)
        row_r, copy_r = arrival(slot, True)
        copy_l.wait_recv()
        copy_r.wait_recv()
        return row_l, row_r

    def first_sweep(row_l, row_r):
        make_scale(row_l)
        make_scale(row_r)
        sweep_rows(p0, p1, [row_l, row_r], send_ghost(p1, land1, 1))

    p1[late_a] = jnp.zeros((BLK, WIDTH), jnp.bfloat16)
    p1[late_b] = jnp.zeros((BLK, WIDTH), jnp.bfloat16)

    def send_slot(slot):
        @pl.when(is_forward(slot))
        def _():
            gather_copy(slot, False, False).start()
            gather_copy(slot, True, False).start()

        @pl.when(jnp.logical_not(is_forward(slot)))
        def _():
            gather_copy(slot, False, True).start()
            gather_copy(slot, True, True).start()

    @pl.loop(0, SLOTS - 1)
    def _(slot):
        rows = receive(slot)

        @pl.when(slot + AHEAD < SLOTS - 2)
        def _():
            send_slot(slot + AHEAD)

        first_sweep(*rows)

        @pl.when((slot >= SLOTS - 4) & (slot < SLOTS - 2))
        def _():
            send_slot(slot + 2)

    def take_ghost(source, landed, sweep, place):
        @pl.when(place < GROUP)
        def _():
            ghost_copy(source, landed, sweep, ROWS - GROUP + place, place, 1, after).wait_recv()

        @pl.when(place >= GROUP)
        def _():
            ghost_copy(source, landed, sweep, place - GROUP, place, 1, before).wait_recv()

        settle(source, landed, place)

    def partial_rows(numbers):
        pairs = [other_pair(number, ROWS // 2 - 4) for number in numbers]

        def finish(number):
            for mxu in range(2):
                partial[2 * pairs[number] + mxu] = pltpu.matmul_pop(acc[2 * (number % 2) + mxu])

        for number, pair in enumerate(pairs):
            product(p1, [(2 * pair, index_a), (2 * pair + 1, index_a)], number % 2)
            if number > 0:
                finish(number - 1)
        finish(len(pairs) - 1)

    late_ghost = jnp.where(me == 2, 2 * GROUP - 4, 0)
    for i in range(4):
        p1[ROWS + late_ghost + i] = jnp.zeros((BLK, WIDTH), jnp.bfloat16)
    partial_rows(range(7))

    @pl.loop(0, 2 * GROUP - 4)
    def _(i):
        take_ghost(p1, land1, 1, i + jnp.where(me == 2, 0, 4))

    partial_rows(range(7, 13))
    first_sweep(*receive(SLOTS - 1))

    send_second = send_ghost(p2, land2, 2)
    sweep_rows(p1, p2, [late_a, late_b], send_second)

    def corrected_rows(numbers):
        pairs = [other_pair(number, 4) for number in numbers]

        def finish(number):
            for mxu in range(2):
                r = 2 * pairs[number] + mxu
                total = partial[r] + pltpu.matmul_pop(acc[2 * (number % 2) + mxu])
                p2[r] = update(p1, r, total)

        tile = jnp.concatenate([p1[late_a], p1[late_b]], axis=0)
        for mxu in range(2):
            pltpu.matmul_push_rhs(tile, 0, mxu)
        for number, pair in enumerate(pairs):
            for mxu in range(2):
                r = 2 * pair + mxu
                k_a, k_b = find_a[r], find_b[r]
                lhs = [held[jnp.where(k < LISTED, r, ROWS), jnp.where(k < LISTED, k, 0)] for k in (k_a, k_b)]
                pltpu.matmul_acc_lhs(
                    acc[2 * (number % 2) + mxu],
                    jnp.concatenate(lhs, axis=1),
                    load_staged_rhs=0 if number == 0 else None,
                )
            if number > 0:
                finish(number - 1)
        finish(len(pairs) - 1)
        if numbers[0] < 7:
            for pair in pairs:
                send_second(2 * pair)
                send_second(2 * pair + 1)

    corrected_rows(range(4))
    corrected_rows(range(4, 7))
    corrected_rows(range(7, 13))

    @pl.loop(0, 4)
    def _(i):
        take_ghost(p1, land1, 1, late_ghost + i)

    sweep_rows(p1, p2, [2 * edge_pair + i for i in range(4)], send_second)

    def put(w, r, value):
        out[w, pl.ds(pl.multiple_of(r * BLK, BLK), BLK), :] = value

    def inner_rows(rows, upper):
        near, far = (2, 0) if upper else (0, 2)

        def finish(number):
            r = rows[number]
            lower_sum = pltpu.matmul_pop(acc[2 * (number % 2)])
            upper_sum = pltpu.matmul_pop(acc[2 * (number % 2) + 1])
            middle = lower_sum[:, BLK:] + upper_sum[:, BLK:]
            near_sum, far_sum = (upper_sum, lower_sum) if upper else (lower_sum, upper_sum)
            factor = scale[r]
            old = p2[r].astype(jnp.float32)
            mask = allow[r]
            put(near, r, jnp.where(mask[:, :BLK] > 0, old[:, :BLK] - factor * near_sum[:, :BLK], 0.0).astype(jnp.bfloat16))
            put(1, r, jnp.where(mask[:, BLK:WIDTH] > 0, old[:, BLK:] - factor * middle, 0.0).astype(jnp.bfloat16))
            put(far, r, jnp.where(mask[:, WIDTH:] > 0, 0.0 - factor * far_sum[:, :BLK], 0.0).astype(jnp.bfloat16))

        for number, r in enumerate(rows):
            product(p2, [(r, index_x), (r, index_y)], number % 2)
            if number > 0:
                finish(number - 1)
        finish(len(rows) - 1)

    for upper in (False, True):
        @pl.loop(ROWS // 2 - GROUP + upper * GROUP, ROWS // 2 + upper * GROUP, step=4)
        def _(r):
            inner_rows([r + i for i in range(4)], upper)

    def outer_rows(rows, outer):
        pairs = [rows[i : i + 2] for i in range(0, len(rows), 2)]

        def finish(number):
            for mxu, r in enumerate(pairs[number]):
                value = update(p2, r, pltpu.matmul_pop(acc[2 * (number % 2) + mxu]))
                put(outer, r, value[:, :BLK])
                put(1, r, value[:, BLK:])

        for number, pair in enumerate(pairs):
            product(p2, [(r, index_a) for r in pair], number % 2)
            if number > 0:
                finish(number - 1)
        finish(len(pairs) - 1)

    @pl.loop(0, 2)
    def _(number):
        upper = jnp.where(me == 2, number, 1 - number)

        @pl.loop(0, GROUP)
        def _(i):
            take_ghost(p2, land2, 2, upper * GROUP + i)

        outer_rows([upper * (ROWS - GROUP) + i for i in range(GROUP)], 2 * upper)

    @pl.loop(0, SLOTS)
    def _(slot):
        @pl.when(is_forward(slot))
        def _():
            gather_copy(slot, False, False).wait_send()
            gather_copy(slot, True, False).wait_send()

        @pl.when(jnp.logical_not(is_forward(slot)))
        def _():
            gather_copy(slot, False, True).wait_send()
            gather_copy(slot, True, True).wait_send()

    @pl.loop(0, GROUP)
    def _(i):
        for source, landed, sweep in ((p1, land1, 1), (p2, land2, 2)):
            ghost_copy(source, landed, sweep, i, GROUP + i, 1, before).wait_send()
            ghost_copy(source, landed, sweep, ROWS - GROUP + i, i, 1, after).wait_send()


def per_device(blocks, a_cols, near_null, owner, p_mask, ghost_send):
    hbm = pl.BlockSpec(memory_space=pltpu.HBM)
    dma = pltpu.SemaphoreType.DMA
    kept = pltpu.VMEM((EMPTY + 1, BLK, WIDTH), jnp.bfloat16)
    landing = pltpu.VMEM((2 * GROUP, BLK, WIDTH), jnp.bfloat16)
    index = pltpu.SMEM((ROWS * LISTED,), jnp.int32)
    result = pl.pallas_call(
        kernel,
        out_shape=pltpu.VMEM((3, ROWS * BLK, BLK), jnp.bfloat16),
        in_specs=[hbm] * 6,
        out_specs=pl.BlockSpec(memory_space=pltpu.VMEM),
        scratch_shapes=[
            pltpu.SMEM((LISTED, ROWS), jnp.int32),
            pltpu.SMEM((ROWS,), jnp.int32),
            pltpu.SMEM((3, 4, ROWS), jnp.int32),
            pltpu.VMEM((ROWS, 32, BLK), jnp.bfloat16),
            dma((4,)),
            pltpu.VMEM((ROWS + 1, LISTED, BLK, BLK), jnp.bfloat16),
            kept,
            kept,
            kept,
            landing,
            landing,
            landing,
            pltpu.VMEM((ROWS, BLK, BLK), jnp.float32),
            pltpu.VMEM((ROWS, 1, 3 * BLK), jnp.int32),
            pltpu.VMEM((ROWS, BLK, WIDTH), jnp.float32),
            pltpu.SMEM((1, 2, GROUP), jnp.int32),
            pltpu.SMEM((1, 2, GROUP), jnp.int32),
            index,
            index,
            index,
            pltpu.SMEM((ROWS,), jnp.int32),
            pltpu.SMEM((ROWS,), jnp.int32),
            dma,
            dma((2, SLOTS)),
            dma((2, SLOTS)),
            dma((2,)),
            dma((2,)),
            dma((3, 2 * GROUP)),
            dma((3, 2 * GROUP)),
        ],
        compiler_params=pltpu.CompilerParams(collective_id=0, has_side_effects=True, vmem_limit_bytes=60 << 20),
        cost_estimate=pl.CostEstimate(flops=10_000_000_000, bytes_accessed=16_000_000, transcendentals=0),
    )(a_cols.T, owner, p_mask.transpose(1, 2, 0), ghost_send, blocks, near_null)
    return result.transpose(1, 0, 2)


def solution(mesh):
    return jax.shard_map(
        per_device,
        mesh=mesh,
        in_specs=(
            P(("dom", "col"), None, None, None),
            P("dom", None),
            P("dom", None, None),
            P("dom"),
            P("dom", None, "col"),
            P("dom", None, None),
        ),
        out_specs=P("dom", None, "col"),
        check_vma=False,
    )
```

```python
import jax
import jax.numpy as jnp
from jax import lax
from jax.experimental import pallas as pl
from jax.experimental.pallas import tpu as pltpu
from jax.sharding import PartitionSpec as P

OMEGA = 2.0 / 3.0
ROWS = 32
LISTED = 8
BLK = 128
COL = 4
GROUP = ROWS // COL
WIDTH = 2 * BLK
EMPTY = ROWS + 2 * GROUP
SLOTS = 12
MESH = pl.DeviceIdType.MESH


def sent_row(group, position, leftward):
    first = 2 * position if not leftward else 2 * position + 1
    second = 2 * position - 7 if not leftward else 2 * position - 8
    place = jnp.where(position < 4, first, second)
    return group * GROUP + jnp.where(group < 2, place, GROUP - 1 - place)


def slot_row(sender, slot, leftward):
    forwards = slot >= GROUP
    source = lax.rem(sender + jnp.where(leftward, 1, COL - 1), COL)
    group = jnp.where(forwards, source, sender)
    position = jnp.where(forwards, slot - GROUP, slot)
    return sent_row(group, position, leftward)


def kernel(
    cols_in, owner_in, mask_at, lists, blocks, vectors_in, out,
    cols, owner, mask_in, vectors, in_sem, held, p0, p1, p2, land0, land1, land2, scale, allow, partial, list_l, list_r, index_a, index_x, index_y, find_a, find_b,
    own_sem, send_sem, recv_sem, list_send, list_recv, ghost_send, ghost_recv,
):
    pl.run_scoped(
        lambda *acc: body(
            cols_in, owner_in, mask_at, lists, blocks, vectors_in, out,
            cols, owner, mask_in, vectors, in_sem, held, p0, p1, p2, land0, land1, land2, scale, allow, partial, list_l, list_r, index_a, index_x, index_y, find_a, find_b,
            own_sem, send_sem, recv_sem, list_send, list_recv, ghost_send, ghost_recv, acc,
        ),
        *[pltpu.ACC(mxu)((BLK, WIDTH), jnp.float32) for _ in range(2) for mxu in range(2)],
    )


def body(
    cols_in, owner_in, mask_at, lists, blocks, vectors_in, out,
    cols, owner, mask_in, vectors, in_sem, held, p0, p1, p2, land0, land1, land2, scale, allow, partial, list_l, list_r, index_a, index_x, index_y, find_a, find_b,
    own_sem, send_sem, recv_sem, list_send, list_recv, ghost_send, ghost_recv, acc,
):
    me = lax.axis_index("col")
    part = lax.axis_index("dom")
    parts = lax.axis_size("dom")
    right, left = lax.rem(me + 1, COL), lax.rem(me + COL - 1, COL)
    after, before = lax.rem(part + 1, parts), lax.rem(part + parts - 1, parts)

    loads = [
        pltpu.make_async_copy(source, target, in_sem.at[number])
        for number, (source, target) in enumerate(
            ((vectors_in, vectors), (owner_in, owner), (mask_at, mask_in), (cols_in, cols))
        )
    ]
    for load in loads:
        load.start()
    barrier = pltpu.get_barrier_semaphore()
    for axis, other in (("col", left), ("col", right), ("dom", before), ("dom", after)):
        pl.semaphore_signal(barrier, inc=1, device_id={axis: other}, device_id_type=MESH)
    pl.semaphore_wait(barrier, 4)

    own_copy = pltpu.make_async_copy(blocks, held.at[pl.ds(me * GROUP, GROUP)], own_sem)

    def gather_copy(slot, leftward, own):
        row = slot_row(me, slot, leftward)
        sem = (1 if leftward else 0), slot
        return pltpu.make_async_remote_copy(
            src_ref=blocks.at[row - me * GROUP] if own else held.at[row],
            dst_ref=held.at[row],
            send_sem=send_sem.at[sem],
            recv_sem=recv_sem.at[sem],
            device_id={"col": left if leftward else right},
            device_id_type=MESH,
        )

    def arrival(slot, leftward):
        row = slot_row(right if leftward else left, slot, leftward)
        sem = (1 if leftward else 0), slot
        return row, pltpu.make_async_remote_copy(
            src_ref=held.at[row],
            dst_ref=held.at[row],
            send_sem=send_sem.at[sem],
            recv_sem=recv_sem.at[sem],
            device_id={"col": left if leftward else right},
            device_id_type=MESH,
        )

    for slot in range(GROUP):
        for leftward in (False, True):
            gather_copy(slot, leftward, True).start()
    own_copy.start()

    def list_copy(here, index, other):
        return pltpu.make_async_remote_copy(
            src_ref=lists,
            dst_ref=here,
            send_sem=list_send.at[index],
            recv_sem=list_recv.at[index],
            device_id={"dom": other},
            device_id_type=MESH,
        )

    list_copy(list_l, 0, after).start()
    list_copy(list_r, 1, before).start()

    def ghost_copy(source, target, sweep, row, place, count, other):
        src = source.at[pl.ds(row, count)] if count > 1 else source.at[row]
        dst = target.at[pl.ds(place, count)] if count > 1 else target.at[place]
        return pltpu.make_async_remote_copy(
            src_ref=src,
            dst_ref=dst,
            send_sem=ghost_send.at[sweep, place],
            recv_sem=ghost_recv.at[sweep, place],
            device_id={"dom": other},
            device_id_type=MESH,
        )

    for load in loads:
        load.wait()

    @pl.loop(0, ROWS)
    def _(r):
        values = vectors[r].astype(jnp.float32)
        tall = jnp.concatenate([values] * 4, axis=0)
        aggregate = lax.broadcasted_iota(jnp.int32, (BLK, BLK), 0) // 32 + me * 4
        owned = jnp.where(aggregate == owner[r], tall, 0.0)
        middle = jnp.transpose(owned).astype(jnp.bfloat16)
        p0[r] = jnp.concatenate([jnp.zeros((BLK, BLK), jnp.bfloat16), middle], axis=1)

    ghost_copy(p0, land0, 0, 0, GROUP, GROUP, before).start()
    ghost_copy(p0, land0, 0, ROWS - GROUP, 0, GROUP, after).start()
    for buffer in (p0, p1, p2):
        buffer[EMPTY] = jnp.zeros((BLK, WIDTH), jnp.bfloat16)
    held[ROWS, 0] = jnp.zeros((BLK, BLK), jnp.bfloat16)
    nothing = jnp.zeros((GROUP * BLK, BLK), jnp.bfloat16)
    out[2, 0 : GROUP * BLK, :] = nothing
    out[0, (ROWS - GROUP) * BLK : ROWS * BLK, :] = nothing

    late_pair = sent_row(lax.rem(me + 2, COL), SLOTS - GROUP - 1, False) // 2
    late_a, late_b = 2 * late_pair, 2 * late_pair + 1
    edge_pair = jnp.where(me == 2, ROWS // 2 - 1, 0)

    def other_pair(number, turn):
        first = lax.rem(late_pair + turn, ROWS // 2)
        second = lax.rem(edge_pair + turn, ROWS // 2)
        low, high = jnp.minimum(first, second), jnp.maximum(first, second)
        place = number + jnp.where(number >= low, 1, 0)
        place = place + jnp.where(place >= high, 1, 0)
        return lax.rem(place + ROWS // 2 - turn, ROWS // 2)

    lane = lax.broadcasted_iota(jnp.int32, (1, BLK), 1) // 32
    for half, order in ((0, (0, 1, 2)), (1, (2, 1, 0))):
        @pl.loop(half * ROWS // 2, (half + 1) * ROWS // 2)
        def _(r):
            pieces = []
            for w in order:
                piece = jnp.zeros((1, BLK), jnp.int32)
                for a in range(4):
                    value = mask_in[w, a, r]
                    if w == 1:
                        value = jnp.where(owner[r] == me * 4 + a, 1, value)
                    piece = jnp.where(lane == a, value, piece)
                pieces.append(piece)
            allow[r] = jnp.concatenate(pieces, axis=1)

    list_copy(list_l, 0, after).wait()
    list_copy(list_r, 1, before).wait()

    @pl.loop(0, ROWS)
    def _(r):
        found_a = jnp.int32(LISTED)
        found_b = jnp.int32(LISTED)
        for k in range(LISTED):
            c = cols[k, r]
            from_left = list_l[0, 1, jnp.clip(c - ROWS, 0, GROUP - 1)] - (ROWS - GROUP)
            from_right = list_r[0, 0, jnp.clip(c - ROWS - GROUP, 0, GROUP - 1)]
            from_left = jnp.where(from_left < 0, EMPTY, from_left + ROWS)
            from_right = jnp.where(from_right < 0, EMPTY, from_right + ROWS + GROUP)
            place = jnp.where(c < ROWS, c, jnp.where(c < ROWS + GROUP, from_left, from_right))
            place = jnp.where(c < 0, EMPTY, place)
            lower = (place < ROWS // 2) | ((place >= ROWS) & (place < ROWS + GROUP))
            index_a[r * LISTED + k] = place
            index_x[r * LISTED + k] = jnp.where(lower, place, EMPTY)
            index_y[r * LISTED + k] = jnp.where(lower, EMPTY, place)
            found_a = jnp.where(place == late_a, k, found_a)
            found_b = jnp.where(place == late_b, k, found_b)
        find_a[r] = found_a
        find_b[r] = found_b

    def settle(target, landed, place):
        value = landed[place]
        value = jnp.concatenate([value[:, BLK:], value[:, :BLK]], axis=1)
        exists = jnp.where(place < GROUP, part > 0, part < parts - 1)
        target[ROWS + place] = jnp.where(exists, value, jnp.zeros_like(value))

    ghost_copy(p0, land0, 0, 0, GROUP, GROUP, before).wait()
    ghost_copy(p0, land0, 0, ROWS - GROUP, 0, GROUP, after).wait()

    @pl.loop(0, 2 * GROUP)
    def _(place):
        settle(p0, land0, place)

    def issue(source, index, r, bank, mxu, q):
        def tile(k):
            return source[index[r * LISTED + k]]

        pltpu.matmul_push_rhs(jnp.concatenate([tile(2 * q), tile(2 * q + 1)], axis=0), q % 2, mxu)

    def multiply(r, bank, mxu, q):
        lhs = jnp.concatenate([held[r, 2 * q], held[r, 2 * q + 1]], axis=1)
        pltpu.matmul_acc_lhs(acc[2 * bank + mxu], lhs, load_staged_rhs=q % 2)

    def product(source, work, bank):
        for q in range(LISTED // 2):
            for mxu, (r, index) in enumerate(work):
                issue(source, index, r, bank, mxu, q)
            for mxu, (r, index) in enumerate(work):
                multiply(r, bank, mxu, q)

    def update(source, r, total):
        factor = scale[r]
        value = source[r].astype(jnp.float32) - jnp.concatenate([factor, factor], axis=1) * total
        return jnp.where(allow[r][:, :WIDTH] > 0, value, 0.0).astype(jnp.bfloat16)

    def make_scale(r):
        diagonal = lax.broadcasted_iota(jnp.int32, (BLK, BLK), 0) == lax.broadcasted_iota(jnp.int32, (BLK, BLK), 1)
        entries = jnp.sum(jnp.where(diagonal, held[r, 0].astype(jnp.float32), 0.0), axis=1, keepdims=True)
        scale[r] = jnp.broadcast_to(OMEGA * (1.0 / entries), (BLK, BLK))

    def sweep_rows(source, target, rows, after_row=None):
        pairs = [rows[i : i + 2] for i in range(0, len(rows), 2)]

        def finish(number):
            for mxu, r in enumerate(pairs[number]):
                target[r] = update(source, r, pltpu.matmul_pop(acc[2 * (number % 2) + mxu]))

        for number, pair in enumerate(pairs):
            product(source, [(r, index_a) for r in pair], number % 2)
            if number > 0:
                finish(number - 1)
        finish(len(pairs) - 1)
        if after_row is not None:
            for r in rows:
                after_row(r)

    def send_ghost(source, landed, sweep):
        def start(r):
            @pl.when(r < GROUP)
            def _():
                ghost_copy(source, landed, sweep, r, GROUP + r, 1, before).start()

            @pl.when(r >= ROWS - GROUP)
            def _():
                ghost_copy(source, landed, sweep, r, r - (ROWS - GROUP), 1, after).start()

        return start

    own_copy.wait()

    @pl.loop(0, GROUP)
    def _(i):
        make_scale(me * GROUP + i)

    sweep_rows(p0, p1, [me * GROUP + i for i in range(GROUP)], send_ghost(p1, land1, 1))

    def receive(slot):
        row_l, copy_l = arrival(slot, False)
        row_r, copy_r = arrival(slot, True)
        copy_l.wait_recv()
        copy_r.wait_recv()
        return row_l, row_r

    def first_sweep(row_l, row_r):
        make_scale(row_l)
        make_scale(row_r)
        sweep_rows(p0, p1, [row_l, row_r], send_ghost(p1, land1, 1))

    p1[late_a] = jnp.zeros((BLK, WIDTH), jnp.bfloat16)
    p1[late_b] = jnp.zeros((BLK, WIDTH), jnp.bfloat16)

    @pl.loop(0, SLOTS - GROUP)
    def _(slot):
        rows = receive(slot)
        gather_copy(slot + GROUP, False, False).start()
        gather_copy(slot + GROUP, True, False).start()
        first_sweep(*rows)

    @pl.loop(SLOTS - GROUP, SLOTS - 1)
    def _(slot):
        first_sweep(*receive(slot))

    def take_ghost(source, landed, sweep, place):
        @pl.when(place < GROUP)
        def _():
            ghost_copy(source, landed, sweep, ROWS - GROUP + place, place, 1, after).wait_recv()

        @pl.when(place >= GROUP)
        def _():
            ghost_copy(source, landed, sweep, place - GROUP, place, 1, before).wait_recv()

        settle(source, landed, place)

    def partial_rows(numbers):
        pairs = [other_pair(number, ROWS // 2 - 4) for number in numbers]

        def finish(number):
            for mxu in range(2):
                partial[2 * pairs[number] + mxu] = pltpu.matmul_pop(acc[2 * (number % 2) + mxu])

        for number, pair in enumerate(pairs):
            product(p1, [(2 * pair, index_a), (2 * pair + 1, index_a)], number % 2)
            if number > 0:
                finish(number - 1)
        finish(len(pairs) - 1)

    late_ghost = jnp.where(me == 2, 2 * GROUP - 2, 0)
    p1[ROWS + late_ghost] = jnp.zeros((BLK, WIDTH), jnp.bfloat16)
    p1[ROWS + late_ghost + 1] = jnp.zeros((BLK, WIDTH), jnp.bfloat16)
    partial_rows(range(7))

    @pl.loop(0, 2 * GROUP - 2, unroll=True)
    def _(i):
        take_ghost(p1, land1, 1, i + jnp.where(me == 2, 0, 2))

    partial_rows(range(7, 14))
    first_sweep(*receive(SLOTS - 1))

    send_second = send_ghost(p2, land2, 2)
    sweep_rows(p1, p2, [late_a, late_b], send_second)

    def corrected_rows(numbers):
        pairs = [other_pair(number, 4) for number in numbers]

        def finish(number):
            for mxu in range(2):
                r = 2 * pairs[number] + mxu
                total = partial[r] + pltpu.matmul_pop(acc[2 * (number % 2) + mxu])
                p2[r] = update(p1, r, total)

        tile = jnp.concatenate([p1[late_a], p1[late_b]], axis=0)
        for mxu in range(2):
            pltpu.matmul_push_rhs(tile, 0, mxu)
        for number, pair in enumerate(pairs):
            for mxu in range(2):
                r = 2 * pair + mxu
                k_a, k_b = find_a[r], find_b[r]
                lhs = [held[jnp.where(k < LISTED, r, ROWS), jnp.where(k < LISTED, k, 0)] for k in (k_a, k_b)]
                pltpu.matmul_acc_lhs(
                    acc[2 * (number % 2) + mxu],
                    jnp.concatenate(lhs, axis=1),
                    load_staged_rhs=0 if number == 0 else None,
                )
            if number > 0:
                finish(number - 1)
        finish(len(pairs) - 1)
        if numbers[0] < 7:
            for pair in pairs:
                send_second(2 * pair)
                send_second(2 * pair + 1)

    corrected_rows(range(4))
    corrected_rows(range(4, 7))
    corrected_rows(range(7, 14))
    take_ghost(p1, land1, 1, late_ghost)
    take_ghost(p1, land1, 1, late_ghost + 1)
    sweep_rows(p1, p2, [2 * edge_pair, 2 * edge_pair + 1], send_second)

    def put(w, r, value):
        out[w, pl.ds(pl.multiple_of(r * BLK, BLK), BLK), :] = value

    def inner_rows(rows, upper):
        near, far = (2, 0) if upper else (0, 2)

        def finish(number):
            r = rows[number]
            lower_sum = pltpu.matmul_pop(acc[2 * (number % 2)])
            upper_sum = pltpu.matmul_pop(acc[2 * (number % 2) + 1])
            middle = lower_sum[:, BLK:] + upper_sum[:, BLK:]
            near_sum, far_sum = (upper_sum, lower_sum) if upper else (lower_sum, upper_sum)
            factor = scale[r]
            old = p2[r].astype(jnp.float32)
            mask = allow[r]
            put(near, r, jnp.where(mask[:, :BLK] > 0, old[:, :BLK] - factor * near_sum[:, :BLK], 0.0).astype(jnp.bfloat16))
            put(1, r, jnp.where(mask[:, BLK:WIDTH] > 0, old[:, BLK:] - factor * middle, 0.0).astype(jnp.bfloat16))
            put(far, r, jnp.where(mask[:, WIDTH:] > 0, 0.0 - factor * far_sum[:, :BLK], 0.0).astype(jnp.bfloat16))

        for number, r in enumerate(rows):
            product(p2, [(r, index_x), (r, index_y)], number % 2)
            if number > 0:
                finish(number - 1)
        finish(len(rows) - 1)

    for upper in (False, True):
        @pl.loop(ROWS // 2 - GROUP + upper * GROUP, ROWS // 2 + upper * GROUP, step=4)
        def _(r):
            inner_rows([r + i for i in range(4)], upper)

    def outer_rows(rows, outer):
        pairs = [rows[i : i + 2] for i in range(0, len(rows), 2)]

        def finish(number):
            for mxu, r in enumerate(pairs[number]):
                value = update(p2, r, pltpu.matmul_pop(acc[2 * (number % 2) + mxu]))
                put(outer, r, value[:, :BLK])
                put(1, r, value[:, BLK:])

        for number, pair in enumerate(pairs):
            product(p2, [(r, index_a) for r in pair], number % 2)
            if number > 0:
                finish(number - 1)
        finish(len(pairs) - 1)

    @pl.loop(0, 2)
    def _(number):
        upper = jnp.where(me == 2, number, 1 - number)

        @pl.loop(0, GROUP, unroll=True)
        def _(i):
            take_ghost(p2, land2, 2, upper * GROUP + i)

        outer_rows([upper * (ROWS - GROUP) + i for i in range(GROUP)], 2 * upper)

    @pl.loop(0, SLOTS)
    def _(slot):
        @pl.when(slot >= GROUP)
        def _():
            gather_copy(slot, False, False).wait_send()
            gather_copy(slot, True, False).wait_send()

        @pl.when(slot < GROUP)
        def _():
            gather_copy(slot, False, True).wait_send()
            gather_copy(slot, True, True).wait_send()

    @pl.loop(0, GROUP)
    def _(i):
        for source, landed, sweep in ((p1, land1, 1), (p2, land2, 2)):
            ghost_copy(source, landed, sweep, i, GROUP + i, 1, before).wait_send()
            ghost_copy(source, landed, sweep, ROWS - GROUP + i, i, 1, after).wait_send()


def per_device(blocks, a_cols, near_null, owner, p_mask, ghost_send):
    hbm = pl.BlockSpec(memory_space=pltpu.HBM)
    dma = pltpu.SemaphoreType.DMA
    kept = pltpu.VMEM((EMPTY + 1, BLK, WIDTH), jnp.bfloat16)
    landing = pltpu.VMEM((2 * GROUP, BLK, WIDTH), jnp.bfloat16)
    index = pltpu.SMEM((ROWS * LISTED,), jnp.int32)
    result = pl.pallas_call(
        kernel,
        out_shape=pltpu.VMEM((3, ROWS * BLK, BLK), jnp.bfloat16),
        in_specs=[hbm] * 6,
        out_specs=pl.BlockSpec(memory_space=pltpu.VMEM),
        scratch_shapes=[
            pltpu.SMEM((LISTED, ROWS), jnp.int32),
            pltpu.SMEM((ROWS,), jnp.int32),
            pltpu.SMEM((3, 4, ROWS), jnp.int32),
            pltpu.VMEM((ROWS, 32, BLK), jnp.bfloat16),
            dma((4,)),
            pltpu.VMEM((ROWS + 1, LISTED, BLK, BLK), jnp.bfloat16),
            kept,
            kept,
            kept,
            landing,
            landing,
            landing,
            pltpu.VMEM((ROWS, BLK, BLK), jnp.float32),
            pltpu.VMEM((ROWS, 1, 3 * BLK), jnp.int32),
            pltpu.VMEM((ROWS, BLK, WIDTH), jnp.float32),
            pltpu.SMEM((1, 2, GROUP), jnp.int32),
            pltpu.SMEM((1, 2, GROUP), jnp.int32),
            index,
            index,
            index,
            pltpu.SMEM((ROWS,), jnp.int32),
            pltpu.SMEM((ROWS,), jnp.int32),
            dma,
            dma((2, SLOTS)),
            dma((2, SLOTS)),
            dma((2,)),
            dma((2,)),
            dma((3, 2 * GROUP)),
            dma((3, 2 * GROUP)),
        ],
        compiler_params=pltpu.CompilerParams(collective_id=0, has_side_effects=True, vmem_limit_bytes=60 << 20),
        cost_estimate=pl.CostEstimate(flops=10_000_000_000, bytes_accessed=16_000_000, transcendentals=0),
    )(a_cols.T, owner, p_mask.transpose(1, 2, 0), ghost_send, blocks, near_null)
    return result.transpose(1, 0, 2)


def solution(mesh):
    return jax.shard_map(
        per_device,
        mesh=mesh,
        in_specs=(
            P(("dom", "col"), None, None, None),
            P("dom", None),
            P("dom", None, None),
            P("dom"),
            P("dom", None, "col"),
            P("dom", None, None),
        ),
        out_specs=P("dom", None, "col"),
        check_vma=False,
    )
```
